128 devices in a mesh: member: 8 (over x, z_hi), space: 16 (over y, z_lo, core).
Axes of the slice: x: 4, y: 4, z: 4 (z_hi: 2, z_lo: 2; z = z_hi * 2 + z_lo), core: 2. Of those that a mesh axis runs over, the one named last changes fastest.
Arguments:
- fields: bfloat16 [8, 100, 65536], P('member', None, 'space'), may hold values from -6 to 6
- target: bfloat16 [100, 65536], P(None, 'space'), may hold values from -6 to 6
- area_weights: float32 [65536], P('space'), may hold values from 0.25 to 5.25, as said below
- hidden: bfloat16 [8, 65536, 1024], P('member', 'space'), may hold values from -6 to 6
- w_in: bfloat16 [1024, 1024], replicated, may hold values from -0.1875 to 0.1875
- w_out: bfloat16 [100, 1024], replicated, may hold values from -0.75 to 0.75
Outputs:
- loss: float32 [], replicated
- grad_hidden: bfloat16 [8, 65536, 1024], P('member', 'space')
- grad_w1: float32 [1024, 1024], P(('member', 'space'))
The draws below stay inside these ranges and needn't reach their ends.
Inputs may be any that keep to these rules, and one draw needn't show every extreme that they name: `area_weights`: positive area weights.
All inputs are finite; a program needn't handle non-finite values.
Results may differ from the reference program's by a relative error of at most 0.0057.
Values may be sent and summed in bfloat16 or wider, within the bound.
A program may use at most 128 MiB of HBM per device.

```python
import math
import jax
import jax.numpy as jnp
from jax import lax

HID = 1024
CHANNELS = 100
MEMBERS = 8
NPOINTS = 65536


def draw_area_weights(key, part):
    key = jax.random.fold_in(key, 5)
    position = jnp.arange(NPOINTS).astype(jnp.float32)
    base = 1.0 + 2.0 * position / (NPOINTS - 1)
    rough = jax.random.uniform(key, (NPOINTS,), jnp.float32, 0.5, 1.5)
    return base * rough


def level_of(rng, extent, cuts, least, top_value):
    def one(dim, shards_of):
        steps = jax.random.uniform(jax.random.fold_in(jax.random.fold_in(rng, 6), dim), (shards_of,), jnp.float32, least / len(cuts), top_value / len(cuts))
        return jnp.repeat(jnp.exp(steps), extent[dim] // shards_of).reshape((-1,) + (1,) * (len(extent) - dim - 1))

    gain = one(*cuts[0])
    for cut in cuts[1:]:
        gain = gain * one(*cut)
    return gain


def noise(own_key, dims, scale, reach, pieces=(), dtype=jnp.bfloat16):
    factor_of = level_of(own_key, dims, pieces, -0.22, 0.18) if pieces else 1.0
    result = jax.random.normal(own_key, dims, jnp.float32) * scale * factor_of
    return jnp.minimum(jnp.maximum(result, -reach), reach).astype(dtype)


def setup_inputs(seed: int = 0) -> dict:
    seeds = jax.random.split(jax.random.key(seed), 7)
    fields = noise(seeds[0], (MEMBERS, CHANNELS, NPOINTS), 1.0, 6.0, ((0, 8), (2, 16)))
    target = noise(seeds[1], (CHANNELS, NPOINTS), 1.0, 6.0, ((1, 16),))
    area_weights = draw_area_weights(jax.random.fold_in(seeds[6], 71), 0)
    hidden = noise(seeds[3], (MEMBERS, NPOINTS, HID), 1.0, 6.0, ((0, 8), (1, 16)))
    w_in = noise(seeds[4], (HID, HID), HID ** -0.5, 0.1875)
    w_out = noise(seeds[5], (CHANNELS, HID), (HID // 16) ** -0.5, 0.75)
    return dict(fields=fields, target=target, area_weights=area_weights, hidden=hidden, w_in=w_in, w_out=w_out)


alpha_fair = 0.95

def gelu_back(pre, upstream):
    return jax.vjp(jax.nn.gelu, pre)[1](upstream)[0]

def reference(fields, target, area_weights, hidden, w_in, w_out):
    count = MEMBERS
    fair = (1.0 - alpha_fair) / count
    coef = (1.0 - fair) / (count * (count - 1))
    values = fields.astype(jnp.float32)
    truth = target.astype(jnp.float32)
    weights = area_weights[None, :]

    def one_member(own):
        gap = own[None] - values
        spread = lax.optimization_barrier(jnp.sum(jnp.abs(gap), 0))
        signs = lax.optimization_barrier(jnp.sum(jnp.sign(gap), 0))
        part = jnp.sum(weights * (jnp.abs(own - truth) / count - 0.5 * coef * spread))
        slope = (weights * jnp.sign(own - truth) / count - coef * weights * signs).astype(jnp.bfloat16)
        return (part, slope)
    parts, slopes = lax.map(one_member, values)
    loss = jnp.sum(parts) / (CHANNELS * NPOINTS)

    def backward(total, item):
        feats, slope = item
        pre = jnp.dot(feats, w_in, preferred_element_type=jnp.float32)
        upstream = lax.dot_general(slope, w_out, (((0,), (0,)), ((), ())), preferred_element_type=jnp.float32)
        delta = gelu_back(pre, upstream).astype(jnp.bfloat16)
        grad_feats = lax.dot_general(delta, w_in, (((1,), (1,)), ((), ())), preferred_element_type=jnp.float32).astype(jnp.bfloat16)
        total = total + lax.dot_general(feats, delta, (((0,), (0,)), ((), ())), preferred_element_type=jnp.float32)
        return (total, grad_feats)
    start = jnp.zeros((HID, HID), jnp.float32)
    total, grad_hidden = lax.scan(backward, start, (hidden, slopes))
    grad_w1 = total * (1.0 / math.sqrt(NPOINTS))
    return (loss, grad_hidden, grad_w1)
```

```python
import functools
import math

import jax
import jax.numpy as jnp
from jax import lax
from jax.experimental import pallas as pl
from jax.experimental.pallas import tpu as pltpu
from jax.sharding import PartitionSpec as P

ALPHA_FAIR = 0.95
MEMBERS, SPACES = 8, 16
CHANNELS, LOCAL, HID = 100, 4096, 1024
PART = LOCAL // MEMBERS
ROOT = math.sqrt(2.0 / math.pi)
CUBIC = 0.044715
F32, BF16 = jnp.float32, jnp.bfloat16
MESH = pl.DeviceIdType.MESH

ORDERS = ((0, 1, 2), (1, 2, 0), (2, 0, 1), (0, 2, 1))
BLOCKS = len(ORDERS)


def gelu_slope(u):
    s = u * u
    t = jnp.tanh(u * (ROOT + (ROOT * CUBIC) * s))
    return 0.5 * (1.0 + t) + (1.0 - t * t) * (u * (0.5 * ROOT + (1.5 * ROOT * CUBIC) * s))


def sign(d):
    return jnp.where(d > 0.0, 1.0, jnp.where(d < 0.0, -1.0, 0.0))


class Place:
    def __init__(self):
        self.member = lax.axis_index("member")
        self.space = lax.axis_index("space")
        x, z_hi = self.member // 2, self.member % 2
        y, z_lo = self.space // 4, (self.space // 2) % 2
        self.core = self.space % 2
        self.at = (x, y, z_hi * 2 + z_lo)

    def far(self, axis, d):
        return (self.at[axis] + d) % 4

    def device(self, at, core):
        x, y, z = at
        return {"member": x * 2 + z // 2, "space": (y * 2 + z % 2) * 2 + core}

    def along(self, axis, d):
        at = list(self.at)
        at[axis] = self.far(axis, d)
        return self.device(at, self.core)

    def other_core(self):
        return self.device(self.at, 1 - self.core)

    def other_member(self, d):
        return {"member": (self.member + d) % MEMBERS, "space": self.space}


def forward_kernel(
    fields, target, area, hidden, w_in, w_out,
    loss_out, du_out, grad_out,
    hid, win, wout, slope, du,
    got, truth, weight, back, dx,
    sums, half0, sum1, part1, sum2, part2, sum3, part3,
    lacc, lsum, lpart,
    local_sem, hid_sem, out_sem, field_sems, back_sems, rs_sems, loss_sems,
):
    here = Place()
    me = here.member
    count = MEMBERS
    fair = (1.0 - ALPHA_FAIR) / count
    coef = (1.0 - fair) / (count * (count - 1))

    mine = pl.ds(pl.multiple_of(me * PART, PART), PART)
    locals_ = [
        pltpu.make_async_copy(src, dst, local_sem.at[i])
        for i, (src, dst) in enumerate((
            (fields.at[0, :, mine], got.at[me]),
            (target.at[:, mine], truth),
            (area.at[:, mine], weight),
            (w_in, win),
            (w_out, wout),
        ))
    ]
    for copy in locals_:
        copy.start()

    def rows_of(c):
        return pl.ds(c * PART, PART)

    loads = [
        pltpu.make_async_copy(hidden.at[0, rows_of(c)], hid.at[rows_of(c)], hid_sem.at[c])
        for c in range(MEMBERS)
    ]
    for copy in loads:
        copy.start()

    barrier = pltpu.get_barrier_semaphore()
    others = [here.other_member(d) for d in range(1, MEMBERS)]
    others += [here.other_core()]
    others += [here.along(1, d) for d in range(1, 4)]
    others += [here.along(2, d) for d in (1, 3)]
    for device in others:
        pl.semaphore_signal(barrier, inc=1, device_id=device, device_id_type=MESH)
    pl.semaphore_wait(barrier, len(others))

    def field_copy(d):
        to = (me + d) % MEMBERS
        return pltpu.make_async_remote_copy(
            src_ref=fields.at[0, :, pl.ds(pl.multiple_of(to * PART, PART), PART)],
            dst_ref=got.at[me],
            send_sem=field_sems.at[0, d - 1],
            recv_sem=field_sems.at[1, d - 1],
            device_id=here.other_member(d),
            device_id_type=MESH,
        )

    def field_arrival(d):
        slot = got.at[(me + MEMBERS - d) % MEMBERS]
        return pltpu.make_async_remote_copy(
            src_ref=slot, dst_ref=slot,
            send_sem=field_sems.at[0, d - 1], recv_sem=field_sems.at[1, d - 1],
            device_id=here.other_member(MEMBERS - d), device_id_type=MESH,
        )

    field_copies = [field_copy(d) for d in range(1, MEMBERS)]
    for copy in field_copies:
        copy.start()

    def project(c):
        loads[c].wait()
        u = jnp.dot(hid[rows_of(c), :], win[...], preferred_element_type=F32)
        slope[rows_of(c), :] = gelu_slope(u)

    locals_[3].wait()
    for c in range(4):
        project(c)

    for copy in locals_[:3]:
        copy.wait()
    for d in range(1, MEMBERS):
        field_arrival(d).wait_recv()
    lacc[...] = jnp.zeros_like(lacc)

    def compare(start, rows):
        at = pl.ds(start, rows)
        for j in range(0, PART, 128):
            lanes = pl.ds(j, 128)
            x = [got[k, at, lanes].astype(F32) for k in range(MEMBERS)]
            y = truth[at, lanes].astype(F32)
            w = weight[:, lanes]
            pull = coef * w
            signs = [0.0] * MEMBERS
            spread = 0.0
            for a in range(MEMBERS):
                for b in range(a + 1, MEMBERS):
                    d = x[a] - x[b]
                    s = sign(d)
                    spread = spread + jnp.abs(d)
                    signs[a] = signs[a] + s
                    signs[b] = signs[b] - s
            miss = 0.0
            for k in range(MEMBERS):
                e = x[k] - y
                miss = miss + jnp.abs(e)
                back[k, at, lanes] = (w * sign(e) / count - pull * signs[k]).astype(BF16)
            lacc[pl.ds(0, rows), :] += w * (miss / count - coef * spread)

    def compare_rows(i, _):
        compare(pl.multiple_of(i * 16, 16), 16)
        return 0

    whole = CHANNELS // 16
    lax.fori_loop(0, whole, compare_rows, 0)
    compare(whole * 16, CHANNELS - whole * 16)

    def back_copy(d):
        to = (me + d) % MEMBERS
        return pltpu.make_async_remote_copy(
            src_ref=back.at[to],
            dst_ref=dx.at[me],
            send_sem=back_sems.at[0, d - 1],
            recv_sem=back_sems.at[1, d - 1],
            device_id=here.other_member(d),
            device_id_type=MESH,
        )

    def back_arrival(d):
        slot = dx.at[(me + MEMBERS - d) % MEMBERS]
        return pltpu.make_async_remote_copy(
            src_ref=slot, dst_ref=slot,
            send_sem=back_sems.at[0, d - 1], recv_sem=back_sems.at[1, d - 1],
            device_id=here.other_member(MEMBERS - d), device_id_type=MESH,
        )

    back_copies = [back_copy(d) for d in range(1, MEMBERS)]
    for copy in back_copies:
        copy.start()
    own_back = pltpu.make_async_copy(back.at[me], dx.at[me], local_sem.at[0])
    own_back.start()

    loss_copies = []

    def loss_send(stage):
        copies = []
        for d in (1,) if stage == 0 else (1, 2, 3):
            k = d - 1 if stage == 0 else 1 + (stage - 1) * 3 + d - 1
            copies.append(pltpu.make_async_remote_copy(
                src_ref=lsum.at[stage],
                dst_ref=lpart.at[k],
                send_sem=loss_sems.at[0, k],
                recv_sem=loss_sems.at[1, k],
                device_id=here.other_core() if stage == 0 else here.along(stage - 1, d),
                device_id_type=MESH,
            ))
        for copy in copies:
            copy.start()
        loss_copies.append(copies)

    def loss_sum(stage):
        total = lsum[stage]
        first = 0 if stage == 0 else 1 + (stage - 1) * 3
        for d, copy in enumerate(loss_copies[stage]):
            copy.wait_recv()
            total = total + lpart[first + d]
        lsum[stage + 1] = total

    lsum[0] = lacc[0:8, :] + lacc[8:16, :]
    loss_send(0)
    for c in range(4, MEMBERS):
        project(c)
        loss_sum(c - 4)
        if c < 7:
            loss_send(c - 3)
    loss_out[0, 0] = jnp.sum(lsum[4]) / (CHANNELS * LOCAL * SPACES)

    locals_[4].wait()
    own_back.wait()
    for d in range(1, MEMBERS):
        back_arrival(d).wait_recv()
    stores = []
    for c in range(MEMBERS):
        dv = lax.dot_general(
            dx[c], wout[...], (((0,), (0,)), ((), ())), preferred_element_type=F32
        )
        du[rows_of(c), :] = (dv * slope[rows_of(c), :]).astype(BF16)
        copy = pltpu.make_async_copy(du.at[rows_of(c)], du_out.at[rows_of(c)], out_sem.at[c])
        copy.start()
        stores.append(copy)

    def weight_grad(h, i):
        g = lax.dot_general(
            hid[:, pl.ds(i * 512, 512)], du[:, pl.ds(h * 512, 512)],
            (((0,), (0,)), ((), ())), preferred_element_type=F32,
        )
        for r in range(64):
            at = (2 * i + r // 32, (r // 4) % 4, ((r // 16) % 2) * 2 + (r // 2) % 2)
            rows = g[8 * r : 8 * r + 8]
            for q in range(2):
                b = 2 * h + q
                p = [at[axis] for axis in ORDERS[b]]
                pair = jnp.concatenate(
                    [rows[:, 256 * q : 256 * q + 128], rows[:, 256 * q + 128 : 256 * q + 256]], 0
                )
                sums[b, r % 2, p[0], p[1], p[2]] = pair.astype(BF16)

    rs_copies = {}

    def rs_send(b, stage):
        copies = []
        if stage == 0:
            copies.append(pltpu.make_async_remote_copy(
                src_ref=sums.at[b, 1 - here.core], dst_ref=half0.at[b],
                send_sem=rs_sems.at[0, b, 0], recv_sem=rs_sems.at[1, b, 0],
                device_id=here.other_core(), device_id_type=MESH,
            ))
        else:
            axis = ORDERS[b][stage - 1]
            src, dst = ((sum1, part1), (sum2, part2), (sum3, part3))[stage - 1]
            for d in (2, 1, 3):
                k = 1 + (stage - 1) * 3 + d - 1
                copies.append(pltpu.make_async_remote_copy(
                    src_ref=src.at[b, here.far(axis, d)], dst_ref=dst.at[b, d - 1],
                    send_sem=rs_sems.at[0, b, k], recv_sem=rs_sems.at[1, b, k],
                    device_id=here.along(axis, d), device_id_type=MESH,
                ))
        for copy in copies:
            copy.start()
        rs_copies[b, stage] = copies

    def rs_sum(b, stage):
        for copy in rs_copies[b, stage]:
            copy.wait_recv()
        if stage == 0:
            for p in range(4):
                sum1[b, p] = (
                    sums[b, here.core, p].astype(F32) + half0[b, p].astype(F32)
                ).astype(BF16)
            return
        src, dst = ((sum1, part1), (sum2, part2), (sum3, part3))[stage - 1]
        total = src[b, here.at[ORDERS[b][stage - 1]]].astype(F32)
        for d in range(3):
            total = total + dst[b, d].astype(F32)
        if stage == 3:
            total = total * (1.0 / math.sqrt(LOCAL * SPACES))
            grad_out[:, pl.ds(256 * b, 128)] = total[0:8]
            grad_out[:, pl.ds(256 * b + 128, 128)] = total[8:16]
        else:
            (sum2, sum3)[stage - 1][b] = total.astype(BF16)

    def step(blocks, stage):
        for b in blocks:
            rs_sum(b, stage)
            if stage < 3:
                rs_send(b, stage + 1)

    early, late = (0, 1), (2, 3)
    weight_grad(0, 0)
    weight_grad(0, 1)
    for b in early:
        rs_send(b, 0)
    weight_grad(1, 0)
    step(early, 0)
    weight_grad(1, 1)
    for b in late:
        rs_send(b, 0)
    step(early, 1)
    step(late, 0)
    step(early, 2)
    step(late, 1)
    step(early, 3)
    step(late, 2)
    step(late, 3)

    for copy in stores:
        copy.wait()
    for copy in field_copies + back_copies:
        copy.wait_send()
    for copies in loss_copies + list(rs_copies.values()):
        for copy in copies:
            copy.wait_send()


def backward_kernel(du, w_in, out):
    out[0] = lax.dot_general(
        du[...], w_in[...], (((1,), (1,)), ((), ())), preferred_element_type=F32
    ).astype(BF16)


def on_device(fields, target, area_weights, hidden, w_in, w_out):
    anywhere = pl.BlockSpec(memory_space=pl.ANY)
    vmem = pl.BlockSpec(memory_space=pltpu.VMEM)
    dma = pltpu.SemaphoreType.DMA
    tile = (16, 128)
    loss, du, grad_w1 = pl.pallas_call(
        forward_kernel,
        out_shape=(
            jax.ShapeDtypeStruct((1, 1), F32),
            jax.ShapeDtypeStruct((LOCAL, HID), BF16),
            jax.ShapeDtypeStruct((8, HID), F32),
        ),
        in_specs=[anywhere] * 6,
        out_specs=(pl.BlockSpec(memory_space=pltpu.SMEM), anywhere, vmem),
        scratch_shapes=[
            pltpu.VMEM((LOCAL, HID), BF16),
            pltpu.VMEM((HID, HID), BF16),
            pltpu.VMEM((CHANNELS, HID), BF16),
            pltpu.VMEM((LOCAL, HID), F32),
            pltpu.VMEM((LOCAL, HID), BF16),
            pltpu.VMEM((MEMBERS, CHANNELS, PART), BF16),
            pltpu.VMEM((CHANNELS, PART), BF16),
            pltpu.VMEM((1, PART), F32),
            pltpu.VMEM((MEMBERS, CHANNELS, PART), BF16),
            pltpu.VMEM((MEMBERS, CHANNELS, PART), BF16),
            pltpu.VMEM((BLOCKS, 2, 4, 4, 4) + tile, BF16),
            pltpu.VMEM((BLOCKS, 4, 4, 4) + tile, BF16),
            pltpu.VMEM((BLOCKS, 4, 4, 4) + tile, BF16),
            pltpu.VMEM((BLOCKS, 3, 4, 4) + tile, BF16),
            pltpu.VMEM((BLOCKS, 4, 4) + tile, BF16),
            pltpu.VMEM((BLOCKS, 3, 4) + tile, BF16),
            pltpu.VMEM((BLOCKS, 4) + tile, BF16),
            pltpu.VMEM((BLOCKS, 3) + tile, BF16),
            pltpu.VMEM((16, 128), F32),
            pltpu.VMEM((5, 8, 128), F32),
            pltpu.VMEM((10, 8, 128), F32),
            dma((5,)),
            dma((MEMBERS,)),
            dma((MEMBERS,)),
            dma((2, MEMBERS - 1)),
            dma((2, MEMBERS - 1)),
            dma((2, BLOCKS, 10)),
            dma((2, 10)),
        ],
        compiler_params=pltpu.CompilerParams(
            collective_id=0, has_side_effects=True, vmem_limit_bytes=60 * 2**20
        ),
        cost_estimate=pl.CostEstimate(
            flops=2 * LOCAL * HID * (2 * HID + CHANNELS), bytes_accessed=24 * 2**20, transcendentals=LOCAL * HID
        ),
    )(fields, target, area_weights[None, :], hidden, w_in, w_out)
    rows = 1024
    grad_hidden = pl.pallas_call(
        backward_kernel,
        out_shape=jax.ShapeDtypeStruct((1, LOCAL, HID), BF16),
        grid=(LOCAL // rows,),
        in_specs=[
            pl.BlockSpec((rows, HID), lambda i: (i, 0)),
            pl.BlockSpec((HID, HID), lambda i: (0, 0)),
        ],
        out_specs=pl.BlockSpec((1, rows, HID), lambda i: (0, i, 0)),
        compiler_params=pltpu.CompilerParams(vmem_limit_bytes=32 * 2**20),
    )(du, w_in)
    return (loss[0, 0], grad_hidden, grad_w1)


def solution(mesh):
    return jax.shard_map(
        on_device,
        mesh=mesh,
        in_specs=(
            P("member", None, "space"),
            P(None, "space"),
            P("space"),
            P("member", "space", None),
            P(),
            P(),
        ),
        out_specs=(P(), P("member", "space", None), P(("member", "space"), None)),
        check_vma=False,
    )
```

```python
import functools
import math

import jax
import jax.numpy as jnp
from jax import lax
from jax.experimental import pallas as pl
from jax.experimental.pallas import tpu as pltpu
from jax.sharding import PartitionSpec as P

ALPHA_FAIR = 0.95
MEMBERS, SPACES = 8, 16
CHANNELS, LOCAL, HID = 100, 4096, 1024
ROOT = math.sqrt(2.0 / math.pi)
CUBIC = 0.044715
F32, BF16 = jnp.float32, jnp.bfloat16
MESH = pl.DeviceIdType.MESH

HALF = LOCAL // 2
SHARE = HALF // MEMBERS
CHUNK = 512

XYZ, YZX, ZXY = (0, 1, 2), (1, 2, 0), (2, 0, 1)
ORDERS = ((XYZ, YZX), (ZXY, XYZ), (YZX, ZXY), (XYZ, YZX))
BLOCKS = len(ORDERS)
COLS = HID // BLOCKS


def gelu_slope(u):
    s = u * u
    t = jnp.tanh(u * (ROOT + (ROOT * CUBIC) * s))
    return 0.5 * (1.0 + t) + (1.0 - t * t) * (u * (0.5 * ROOT + (1.5 * ROOT * CUBIC) * s))


def sign(a, b):
    one, zero = jnp.ones((), a.dtype), jnp.zeros((), a.dtype)
    return jnp.where(a > b, one, jnp.where(a < b, -one, zero))


class Place:
    def __init__(self):
        self.member = lax.axis_index("member")
        self.space = lax.axis_index("space")
        x, z_hi = self.member // 2, self.member % 2
        y, z_lo = self.space // 4, (self.space // 2) % 2
        self.core = self.space % 2
        self.at = (x, y, z_hi * 2 + z_lo)

    def pick(self, block, stage):
        first, second = (ORDERS[block][c][stage - 1] for c in (0, 1))
        return [
            (1 - self.core) * int(first == axis) + self.core * int(second == axis)
            for axis in range(3)
        ]

    def slot(self, weights, d=0):
        return (sum(w * p for w, p in zip(weights, self.at)) + d) % 4

    def step(self, weights, d):
        at = [(p + w * d) % 4 for w, p in zip(weights, self.at)]
        return self.device(at, self.core)

    def device(self, at, core):
        x, y, z = at
        return {"member": x * 2 + z // 2, "space": (y * 2 + z % 2) * 2 + core}

    def along(self, axis, d):
        return self.step([int(axis == i) for i in range(3)], d)

    def other_core(self):
        return self.device(self.at, 1 - self.core)

    def other_member(self, d):
        return {"member": (self.member + d) % MEMBERS, "space": self.space}


def forward_kernel(
    fields, target, area, hidden, w_in, w_out,
    loss_out, held, grad_out,
    win, wout, pre0, pre1, slope, du, total,
    got, truth, weight, back, dx,
    sums, half0, sum1, part1, sum2, part2, sum3, part3,
    lacc, lsum, lpart,
    local_sems, own_sems, hid_sems, field_sems, back_sems, rs_sems, loss_sems,
):
    here = Place()
    me = here.member
    count = MEMBERS
    fair = (1.0 - ALPHA_FAIR) / count
    coef = (1.0 - fair) / (count * (count - 1))

    def share(h, member):
        return pl.ds(pl.multiple_of(h * HALF + member * SHARE, SHARE), SHARE)

    def chunk(c):
        return pl.ds(c * CHUNK, CHUNK)

    loads = [
        pltpu.make_async_copy(hidden.at[0, chunk(c)], held.at[chunk(c)], hid_sems.at[c])
        for c in range(LOCAL // CHUNK)
    ]
    weights = [
        pltpu.make_async_copy(src, dst, local_sems.at[i])
        for i, (src, dst) in enumerate(((w_in, win), (w_out, wout)))
    ]
    own = [
        [
            pltpu.make_async_copy(src, dst, own_sems.at[h, i])
            for i, (src, dst) in enumerate((
                (fields.at[0, :, share(h, me)], got.at[h, me]),
                (target.at[:, share(h, me)], truth.at[h]),
                (area.at[:, share(h, me)], weight.at[h]),
            ))
        ]
        for h in range(2)
    ]
    for copy in [weights[0], *loads[:2], *own[0], *loads[2:], weights[1], *own[1]]:
        copy.start()

    barrier = pltpu.get_barrier_semaphore()
    others = [here.other_member(d) for d in range(1, MEMBERS)]
    others += [here.other_core()]
    others += [here.along(1, d) for d in range(1, 4)]
    others += [here.along(2, d) for d in (1, 3)]
    for device in others:
        pl.semaphore_signal(barrier, inc=1, device_id=device, device_id_type=MESH)

    pre = (pre0, pre1)

    def project(c):
        if c < len(loads):
            loads[c].wait()
            pre[c % 2][...] = jnp.dot(held[chunk(c), :], win[...], preferred_element_type=F32)
        if c > 0:
            slope[chunk(c - 1), :] = gelu_slope(pre[(c - 1) % 2][...])

    weights[0].wait()
    project(0)
    pl.semaphore_wait(barrier, len(others))

    def exchange(h, sems, source, landed):
        sent = [
            pltpu.make_async_remote_copy(
                src_ref=source((me + d) % MEMBERS),
                dst_ref=landed.at[h, me],
                send_sem=sems.at[0, h, d - 1],
                recv_sem=sems.at[1, h, d - 1],
                device_id=here.other_member(d),
                device_id_type=MESH,
            )
            for d in range(1, MEMBERS)
        ]
        for copy in sent:
            copy.start()
        return sent

    def arrive(h, sems, landed):
        for d in range(1, MEMBERS):
            slot = landed.at[h, (me + MEMBERS - d) % MEMBERS]
            pltpu.make_async_remote_copy(
                src_ref=slot, dst_ref=slot,
                send_sem=sems.at[0, h, d - 1], recv_sem=sems.at[1, h, d - 1],
                device_id=here.other_member(MEMBERS - d), device_id_type=MESH,
            ).wait_recv()

    sent = []

    def send_fields(h):
        sent.extend(exchange(h, field_sems, lambda to: fields.at[0, :, share(h, to)], got))

    def send_back(h):
        sent.extend(exchange(h, back_sems, lambda to: back.at[h, to], dx))
        copy = pltpu.make_async_copy(back.at[h, me], dx.at[h, me], own_sems.at[h, 0])
        copy.start()
        return copy

    def compare(h, start, rows):
        at = pl.ds(start, rows)
        for j in range(0, SHARE, 128):
            lanes = pl.ds(j, 128)
            x = [got[h, k, at, lanes] for k in range(MEMBERS)]
            y = truth[h, at, lanes]
            w = weight[h, :, lanes]
            pull = coef * w
            push = w / count
            signs = [None] * MEMBERS
            for a in range(MEMBERS):
                for b in range(a + 1, MEMBERS):
                    s = sign(x[a], x[b])
                    signs[a] = s if signs[a] is None else signs[a] + s
                    signs[b] = -s if signs[b] is None else signs[b] - s
            truth_ = y.astype(F32)
            spread, miss = 0.0, 0.0
            for k in range(MEMBERS):
                own_, tally = x[k].astype(F32), signs[k].astype(F32)
                spread = spread + own_ * tally
                miss = miss + jnp.abs(own_ - truth_)
                side = sign(own_, truth_)
                back[h, k, at, lanes] = (push * side - pull * tally).astype(BF16)
            lacc[pl.ds(0, rows), :] += w * (miss / count - coef * spread)

    def compare_half(h):
        for copy in own[h]:
            copy.wait()
        arrive(h, field_sems, got)

        def rows16(i, _):
            compare(h, pl.multiple_of(i * 16, 16), 16)
            return 0

        whole = CHANNELS // 16
        lax.fori_loop(0, whole, rows16, 0)
        compare(h, whole * 16, CHANNELS - whole * 16)

    def upstream(h):
        arrive(h, back_sems, dx)
        for k in range(MEMBERS):
            rows = pl.ds(h * HALF + k * SHARE, SHARE)
            dv = lax.dot_general(
                dx[h, k], wout[...], (((0,), (0,)), ((), ())), preferred_element_type=F32
            )
            du[rows, :] = (dv * slope[rows, :]).astype(BF16)

    def weight_grad(h, cols):
        points = pl.ds(h * HALF, HALF)
        return lax.dot_general(
            held[points, :], du[points, cols], (((0,), (0,)), ((), ())), preferred_element_type=F32
        )

    rs_copies = {}

    def rs_send(b, stage):
        copies = []
        if stage == 0:
            copies.append(pltpu.make_async_remote_copy(
                src_ref=sums.at[b, 1 - here.core], dst_ref=half0.at[b],
                send_sem=rs_sems.at[0, b, 0], recv_sem=rs_sems.at[1, b, 0],
                device_id=here.other_core(), device_id_type=MESH,
            ))
        else:
            axis = here.pick(b, stage)
            src, dst = ((sum1, part1), (sum2, part2), (sum3, part3))[stage - 1]
            for d in (2, 1, 3):
                k = 1 + (stage - 1) * 3 + d - 1
                copies.append(pltpu.make_async_remote_copy(
                    src_ref=src.at[b, here.slot(axis, d)], dst_ref=dst.at[b, d - 1],
                    send_sem=rs_sems.at[0, b, k], recv_sem=rs_sems.at[1, b, k],
                    device_id=here.step(axis, d), device_id_type=MESH,
                ))
        for copy in copies:
            copy.start()
        rs_copies[b, stage] = copies

    def rs_sum(b, stage):
        for copy in rs_copies[b, stage]:
            copy.wait_recv()
        if stage == 0:
            for p in range(4):
                sum1[b, p] = (
                    sums[b, here.core, p].astype(F32) + half0[b, p].astype(F32)
                ).astype(BF16)
            return
        src, dst = ((sum1, part1), (sum2, part2), (sum3, part3))[stage - 1]
        value = src[b, here.slot(here.pick(b, stage))].astype(F32)
        for d in range(3):
            value = value + dst[b, d].astype(F32)
        if stage == 3:
            value = value * (1.0 / math.sqrt(LOCAL * SPACES))
            grad_out[:, pl.ds(COLS * b, 128)] = value[0:8]
            grad_out[:, pl.ds(COLS * b + 128, 128)] = value[8:16]
        else:
            (sum2, sum3)[stage - 1][b] = value.astype(BF16)

    def step(b, stage):
        rs_sum(b, stage)
        if stage < 3:
            rs_send(b, stage + 1)

    loss_copies = []

    def loss_send(stage):
        copies = []
        for d in (1,) if stage == 0 else (1, 2, 3):
            k = d - 1 if stage == 0 else 1 + (stage - 1) * 3 + d - 1
            copies.append(pltpu.make_async_remote_copy(
                src_ref=lsum.at[stage],
                dst_ref=lpart.at[k],
                send_sem=loss_sems.at[0, k],
                recv_sem=loss_sems.at[1, k],
                device_id=here.other_core() if stage == 0 else here.along(stage - 1, d),
                device_id_type=MESH,
            ))
        for copy in copies:
            copy.start()
        loss_copies.append(copies)

    def loss_step(stage):
        value = lsum[stage]
        first = 0 if stage == 0 else 1 + (stage - 1) * 3
        for d, copy in enumerate(loss_copies[stage]):
            copy.wait_recv()
            value = value + lpart[first + d]
        lsum[stage + 1] = value
        if stage < 3:
            loss_send(stage + 1)

    lacc[...] = jnp.zeros_like(lacc)
    send_fields(0)
    project(1)
    project(2)
    send_fields(1)
    project(3)
    project(4)
    compare_half(0)
    own_back0 = send_back(0)
    project(5)
    project(6)
    compare_half(1)
    own_back1 = send_back(1)
    project(7)
    project(8)
    weights[1].wait()
    own_back0.wait()
    upstream(0)

    def first_half(j, _):
        cols = pl.ds(pl.multiple_of(j * COLS, COLS), COLS)
        total[:, cols] = weight_grad(0, cols)
        return 0

    lax.fori_loop(0, BLOCKS, first_half, 0)
    own_back1.wait()
    upstream(1)
    lsum[0] = lacc[0:8, :] + lacc[8:16, :]
    for b in range(BLOCKS):
        cols = pl.ds(b * COLS, COLS)
        g = total[:, cols] + weight_grad(1, cols)
        for r in range(HID // 8):
            core = r % 2
            at = (r // 32, (r // 4) % 4, ((r // 16) % 2) * 2 + (r // 2) % 2)
            i, j, k = (at[axis] for axis in ORDERS[b][core])
            rows = g[8 * r : 8 * r + 8]
            sums[b, core, i, j, k] = jnp.concatenate([rows[:, :128], rows[:, 128:]], 0).astype(BF16)
        rs_send(b, 0)
        if b == 0:
            loss_send(0)
        else:
            step(b - 1, 0)
            if b == 1:
                loss_step(0)

    def grad_hidden(c):
        held[chunk(c), :] = lax.dot_general(
            du[chunk(c), :], win[...], (((1,), (1,)), ((), ())), preferred_element_type=F32
        ).astype(BF16)

    between = (
        ((3, 0),),
        ((0, 1),),
        ((1, 1),),
        ((2, 1),),
        ((3, 1), (0, 2)),
        ((1, 2), (2, 2)),
        ((3, 2), (0, 3)),
        ((1, 3), (2, 3), (3, 3)),
    )
    for c, steps in enumerate(between):
        grad_hidden(c)
        for b, stage in steps:
            step(b, stage)
            if b == 0:
                loss_step(stage)
    loss_out[0, 0] = jnp.sum(lsum[4]) / (CHANNELS * LOCAL * SPACES)

    for copy in sent:
        copy.wait_send()
    for copies in loss_copies + list(rs_copies.values()):
        for copy in copies:
            copy.wait_send()


def store_kernel(grad_hidden, grad_w1, hidden_out, w1_out, sems):
    copies = [
        pltpu.make_async_copy(
            grad_hidden.at[pl.ds(i * HALF, HALF)], hidden_out.at[0, pl.ds(i * HALF, HALF)], sems.at[i]
        )
        for i in range(2)
    ]
    copies.append(pltpu.make_async_copy(grad_w1, w1_out, sems.at[2]))
    for copy in copies:
        copy.start()
    for copy in copies:
        copy.wait()


def on_device(fields, target, area_weights, hidden, w_in, w_out):
    anywhere = pl.BlockSpec(memory_space=pl.ANY)
    vmem = pl.BlockSpec(memory_space=pltpu.VMEM)
    dma = pltpu.SemaphoreType.DMA
    tile = (16, 128)
    loss, grad_hidden, grad_w1 = pl.pallas_call(
        forward_kernel,
        out_shape=(
            jax.ShapeDtypeStruct((1, 1), F32),
            pltpu.VMEM((LOCAL, HID), BF16),
            pltpu.VMEM((8, HID), F32),
        ),
        in_specs=[anywhere] * 6,
        out_specs=(pl.BlockSpec(memory_space=pltpu.SMEM), vmem, vmem),
        scratch_shapes=[
            pltpu.VMEM((HID, HID), BF16),
            pltpu.VMEM((CHANNELS, HID), BF16),
            pltpu.VMEM((CHUNK, HID), F32),
            pltpu.VMEM((CHUNK, HID), F32),
            pltpu.VMEM((LOCAL, HID), F32),
            pltpu.VMEM((LOCAL, HID), BF16),
            pltpu.VMEM((HID, HID), F32),
            pltpu.VMEM((2, MEMBERS, CHANNELS, SHARE), BF16),
            pltpu.VMEM((2, CHANNELS, SHARE), BF16),
            pltpu.VMEM((2, 1, SHARE), F32),
            pltpu.VMEM((2, MEMBERS, CHANNELS, SHARE), BF16),
            pltpu.VMEM((2, MEMBERS, CHANNELS, SHARE), BF16),
            pltpu.VMEM((BLOCKS, 2, 4, 4, 4) + tile, BF16),
            pltpu.VMEM((BLOCKS, 4, 4, 4) + tile, BF16),
            pltpu.VMEM((BLOCKS, 4, 4, 4) + tile, BF16),
            pltpu.VMEM((BLOCKS, 3, 4, 4) + tile, BF16),
            pltpu.VMEM((BLOCKS, 4, 4) + tile, BF16),
            pltpu.VMEM((BLOCKS, 3, 4) + tile, BF16),
            pltpu.VMEM((BLOCKS, 4) + tile, BF16),
            pltpu.VMEM((BLOCKS, 3) + tile, BF16),
            pltpu.VMEM((16, 128), F32),
            pltpu.VMEM((5, 8, 128), F32),
            pltpu.VMEM((10, 8, 128), F32),
            dma((2,)),
            dma((2, 3)),
            dma((LOCAL // CHUNK,)),
            dma((2, 2, MEMBERS - 1)),
            dma((2, 2, MEMBERS - 1)),
            dma((2, BLOCKS, 10)),
            dma((2, 10)),
        ],
        compiler_params=pltpu.CompilerParams(
            collective_id=0, has_side_effects=True, vmem_limit_bytes=52 * 2**20
        ),
        cost_estimate=pl.CostEstimate(
            flops=2 * LOCAL * HID * (3 * HID + CHANNELS),
            bytes_accessed=12 * 2**20,
            transcendentals=LOCAL * HID,
        ),
    )(fields, target, area_weights[None, :], hidden, w_in, w_out)
    grad_hidden, grad_w1 = pl.pallas_call(
        store_kernel,
        out_shape=(
            jax.ShapeDtypeStruct((1, LOCAL, HID), BF16),
            jax.ShapeDtypeStruct((8, HID), F32),
        ),
        in_specs=[anywhere] * 2,
        out_specs=(anywhere, anywhere),
        scratch_shapes=[dma((3,))],
    )(grad_hidden, grad_w1)
    return (loss[0, 0], grad_hidden, grad_w1)


def solution(mesh):
    return jax.shard_map(
        on_device,
        mesh=mesh,
        in_specs=(
            P("member", None, "space"),
            P(None, "space"),
            P("space"),
            P("member", "space", None),
            P(),
            P(),
        ),
        out_specs=(P(), P("member", "space", None), P(("member", "space"), None)),
        check_vma=False,
    )
```

```python
import functools
import math

import jax
import jax.numpy as jnp
from jax import lax
from jax.experimental import pallas as pl
from jax.experimental.pallas import tpu as pltpu
from jax.sharding import PartitionSpec as P

ALPHA_FAIR = 0.95
MEMBERS, SPACES = 8, 16
CHANNELS, LOCAL, HID = 100, 4096, 1024
ROOT = math.sqrt(2.0 / math.pi)
CUBIC = 0.044715
F32, BF16 = jnp.float32, jnp.bfloat16
MESH = pl.DeviceIdType.MESH

HALF = LOCAL // 2
SHARE = HALF // MEMBERS
CHUNK = 512

BLOCKS = 4
COLS = HID // BLOCKS


def gelu_slope(u):
    s = u * u
    t = jnp.tanh(u * (ROOT + (ROOT * CUBIC) * s))
    return 0.5 * (1.0 + t) + (1.0 - t * t) * (u * (0.5 * ROOT + (1.5 * ROOT * CUBIC) * s))


def sign(a, b):
    one, zero = jnp.ones((), a.dtype), jnp.zeros((), a.dtype)
    return jnp.where(a > b, one, jnp.where(a < b, -one, zero))


class Place:
    def __init__(self):
        self.member = lax.axis_index("member")
        self.space = lax.axis_index("space")
        x, z_hi = self.member // 2, self.member % 2
        y, z_lo = self.space // 4, (self.space // 2) % 2
        self.core = self.space % 2
        self.at = (x, y, z_hi * 2 + z_lo)

    def pick(self, block, stage):
        axis = (2 * block + self.core + stage - 1) % 3
        return [(2 - axis) * (1 - axis) // 2, axis * (2 - axis), axis * (axis - 1) // 2]

    def slot(self, weights, d=0):
        return (sum(w * p for w, p in zip(weights, self.at)) + d) % 4

    def step(self, weights, d):
        at = [(p + w * d) % 4 for w, p in zip(weights, self.at)]
        return self.device(at, self.core)

    def device(self, at, core):
        x, y, z = at
        return {"member": x * 2 + z // 2, "space": (y * 2 + z % 2) * 2 + core}

    def along(self, axis, d):
        return self.step([int(axis == i) for i in range(3)], d)

    def other_core(self):
        return self.device(self.at, 1 - self.core)

    def other_member(self, d):
        return {"member": (self.member + d) % MEMBERS, "space": self.space}


def forward_kernel(
    fields, target, area, hidden, w_in, w_out,
    loss_out, held, grad_out,
    win, wout, slope, du, total,
    got, truth, weight, back, dx,
    sums, half0, sum1, part1, sum2, part2, sum3, part3,
    lacc, lsum, lpart,
    local_sems, own_sems, hid_sems, field_sems, back_sems, rs_sems, loss_sems,
):
    here = Place()
    me = here.member
    count = MEMBERS
    fair = (1.0 - ALPHA_FAIR) / count
    coef = (1.0 - fair) / (count * (count - 1))

    def share(h, member):
        return pl.ds(pl.multiple_of(h * HALF + member * SHARE, SHARE), SHARE)

    def chunk(c):
        return pl.ds(pl.multiple_of(c * CHUNK, CHUNK), CHUNK)

    def load(c):
        rows = pl.ds(pl.multiple_of(c * CHUNK, CHUNK), CHUNK)
        return pltpu.make_async_copy(hidden.at[0, rows], held.at[rows], hid_sems.at[c])

    loads = [load(c) for c in range(LOCAL // CHUNK)]
    weights = [
        pltpu.make_async_copy(src, dst, local_sems.at[i])
        for i, (src, dst) in enumerate(((w_in, win), (w_out, wout)))
    ]
    def own_copies(h):
        return [
            pltpu.make_async_copy(src, dst, own_sems.at[h, i])
            for i, (src, dst) in enumerate((
                (fields.at[0, :, share(h, me)], got.at[h, me]),
                (target.at[:, share(h, me)], truth.at[h]),
                (area.at[:, share(h, me)], weight.at[h]),
            ))
        ]

    for copy in [weights[0], *loads[:2], *own_copies(0), *loads[2:], weights[1], *own_copies(1)]:
        copy.start()

    barrier = pltpu.get_barrier_semaphore()
    others = [here.other_member(d) for d in range(1, MEMBERS)]
    others += [here.other_core()]
    others += [here.along(1, d) for d in range(1, 4)]
    others += [here.along(2, d) for d in (1, 3)]
    for device in others:
        pl.semaphore_signal(barrier, inc=1, device_id=device, device_id_type=MESH)

    def project(first, last):
        for c in range(first, last):
            loads[c].wait()

        def one_chunk(c, _):
            u = jnp.dot(held[chunk(c), :], win[...], preferred_element_type=F32)
            slope[chunk(c), :] = gelu_slope(u)
            return 0

        lax.fori_loop(first, last, one_chunk, 0)

    lacc[...] = jnp.zeros_like(lacc)
    weights[0].wait()
    project(0, 1)
    pl.semaphore_wait(barrier, len(others))

    def exchange(h, sems, source, landed):
        return [
            pltpu.make_async_remote_copy(
                src_ref=source((me + d) % MEMBERS),
                dst_ref=landed.at[h, me],
                send_sem=sems.at[0, h, d - 1],
                recv_sem=sems.at[1, h, d - 1],
                device_id=here.other_member(d),
                device_id_type=MESH,
            )
            for d in range(1, MEMBERS)
        ]

    def arrive(h, sems, landed):
        for d in range(1, MEMBERS):
            slot = landed.at[h, (me + MEMBERS - d) % MEMBERS]
            pltpu.make_async_remote_copy(
                src_ref=slot, dst_ref=slot,
                send_sem=sems.at[0, h, d - 1], recv_sem=sems.at[1, h, d - 1],
                device_id=here.other_member(MEMBERS - d), device_id_type=MESH,
            ).wait_recv()

    def field_copies(h):
        return exchange(h, field_sems, lambda to: fields.at[0, :, share(h, to)], got)

    def back_copies(h):
        return exchange(h, back_sems, lambda to: back.at[h, to], dx)

    def own_back(h):
        return pltpu.make_async_copy(back.at[h, me], dx.at[h, me], own_sems.at[h, 0])

    def compare(h, start, rows):
        at = pl.ds(start, rows)
        for j in range(0, SHARE, 128):
            lanes = pl.ds(j, 128)
            x = [got[h, k, at, lanes] for k in range(MEMBERS)]
            y = truth[h, at, lanes]
            w = weight[h, :, lanes]
            pull = coef * w
            push = w / count
            signs = [None] * MEMBERS
            for a in range(MEMBERS):
                for b in range(a + 1, MEMBERS):
                    s = sign(x[a], x[b])
                    signs[a] = s if signs[a] is None else signs[a] + s
                    signs[b] = -s if signs[b] is None else signs[b] - s
            truth_ = y.astype(F32)
            spread, miss = 0.0, 0.0
            for k in range(MEMBERS):
                own_, tally = x[k].astype(F32), signs[k].astype(F32)
                spread = spread + own_ * tally
                miss = miss + jnp.abs(own_ - truth_)
                side = sign(own_, truth_)
                back[h, k, at, lanes] = (push * side - pull * tally).astype(BF16)
            lacc[pl.ds(0, rows), :] += w * (miss / count - coef * spread)

    def compare_half(h):
        for copy in own_copies(h):
            copy.wait()
        arrive(h, field_sems, got)

        def rows16(i, _):
            compare(h, pl.multiple_of(i * 16, 16), 16)
            return 0

        whole = CHANNELS // 16
        lax.fori_loop(0, whole, rows16, 0)
        compare(h, whole * 16, CHANNELS - whole * 16)
        for copy in (own_back(h), *back_copies(h)):
            copy.start()

    def upstream(h):
        own_back(h).wait()
        arrive(h, back_sems, dx)

        for k in range(MEMBERS):
            rows = pl.ds(h * HALF + k * SHARE, SHARE)
            dv = lax.dot_general(
                dx[h, k], wout[...], (((0,), (0,)), ((), ())), preferred_element_type=F32
            )
            du[rows, :] = (dv * slope[rows, :]).astype(BF16)

    def weight_grad(h, b):
        points, cols = pl.ds(h * HALF, HALF), pl.ds(b * COLS, COLS)
        return lax.dot_general(
            held[points, :], du[points, cols], (((0,), (0,)), ((), ())), preferred_element_type=F32
        )

    def pack(b, g):
        for r in range(HID // 8):
            core = r % 2
            at = (r // 32, (r // 4) % 4, ((r // 16) % 2) * 2 + (r // 2) % 2)
            i, j, k = (at[(2 * b + core + s) % 3] for s in range(3))
            rows = g[8 * r : 8 * r + 8]
            sums[b, core, i, j, k] = jnp.concatenate([rows[:, :128], rows[:, 128:]], 0).astype(BF16)

    def rs_copies(b, stage):
        if stage == 0:
            return [pltpu.make_async_remote_copy(
                src_ref=sums.at[b, 1 - here.core], dst_ref=half0.at[b],
                send_sem=rs_sems.at[0, b, 0], recv_sem=rs_sems.at[1, b, 0],
                device_id=here.other_core(), device_id_type=MESH,
            )]
        axis = here.pick(b, stage)
        src, dst = ((sum1, part1), (sum2, part2), (sum3, part3))[stage - 1]
        copies = []
        for d in (2, 1, 3):
            k = 1 + (stage - 1) * 3 + d - 1
            copies.append(pltpu.make_async_remote_copy(
                src_ref=src.at[b, here.slot(axis, d)], dst_ref=dst.at[b, d - 1],
                send_sem=rs_sems.at[0, b, k], recv_sem=rs_sems.at[1, b, k],
                device_id=here.step(axis, d), device_id_type=MESH,
            ))
        return copies

    def rs_send(b, stage):
        for copy in rs_copies(b, stage):
            copy.start()

    def rs_sum(b, stage):
        for copy in rs_copies(b, stage):
            copy.wait_recv()
        if stage == 0:
            for p in range(4):
                sum1[b, p] = (
                    sums[b, here.core, p].astype(F32) + half0[b, p].astype(F32)
                ).astype(BF16)
            return
        src, dst = ((sum1, part1), (sum2, part2), (sum3, part3))[stage - 1]
        value = src[b, here.slot(here.pick(b, stage))].astype(F32)
        for d in range(3):
            value = value + dst[b, d].astype(F32)
        if stage == 3:
            value = value * (1.0 / math.sqrt(LOCAL * SPACES))
            grad_out[:, pl.ds(COLS * b, 128)] = value[0:8]
            grad_out[:, pl.ds(COLS * b + 128, 128)] = value[8:16]
        else:
            (sum2, sum3)[stage - 1][b] = value.astype(BF16)

    def step(b, stage):
        rs_sum(b, stage)
        if stage < 3:
            rs_send(b, stage + 1)

    def loss_copies(stage):
        copies = []
        for d in (1,) if stage == 0 else (1, 2, 3):
            k = d - 1 if stage == 0 else 1 + (stage - 1) * 3 + d - 1
            copies.append(pltpu.make_async_remote_copy(
                src_ref=lsum.at[stage],
                dst_ref=lpart.at[k],
                send_sem=loss_sems.at[0, k],
                recv_sem=loss_sems.at[1, k],
                device_id=here.other_core() if stage == 0 else here.along(stage - 1, d),
                device_id_type=MESH,
            ))
        return copies

    def loss_send(stage):
        for copy in loss_copies(stage):
            copy.start()

    def loss_step(stage):
        value = lsum[stage]
        first = 0 if stage == 0 else 1 + (stage - 1) * 3
        for d, copy in enumerate(loss_copies(stage)):
            copy.wait_recv()
            value = value + lpart[first + d]
        lsum[stage + 1] = value
        if stage < 3:
            loss_send(stage + 1)

    for copy in field_copies(0):
        copy.start()
    project(1, 3)
    for copy in field_copies(1):
        copy.start()
    project(3, 5)
    compare_half(0)
    project(5, 7)
    compare_half(1)
    project(7, 8)
    weights[1].wait()
    upstream(0)
    for b in range(BLOCKS):
        total[:, pl.ds(b * COLS, COLS)] = weight_grad(0, b)
    upstream(1)
    lsum[0] = lacc[0:8, :] + lacc[8:16, :]
    for b in range(BLOCKS):
        pack(b, total[:, pl.ds(b * COLS, COLS)] + weight_grad(1, b))
        rs_send(b, 0)
        if b == 0:
            loss_send(0)
        else:
            step(b - 1, 0)
        if b == 1:
            loss_step(0)
    between = (
        ((3, 0),),
        ((0, 1),),
        ((1, 1),),
        ((2, 1),),
        ((3, 1), (0, 2)),
        ((1, 2), (2, 2)),
        ((3, 2), (0, 3)),
        ((1, 3), (2, 3), (3, 3)),
    )

    for c, steps in enumerate(between):
        held[chunk(c), :] = lax.dot_general(
            du[chunk(c), :], win[...], (((1,), (1,)), ((), ())), preferred_element_type=F32
        ).astype(BF16)
        for b, stage in steps:
            step(b, stage)
            if b == 0:
                loss_step(stage)
    loss_out[0, 0] = jnp.sum(lsum[4]) / (CHANNELS * LOCAL * SPACES)

    for h in range(2):
        for copy in field_copies(h) + back_copies(h):
            copy.wait_send()
    for stage in range(4):
        for copy in loss_copies(stage):
            copy.wait_send()
        for b in range(BLOCKS):
            for copy in rs_copies(b, stage):
                copy.wait_send()


def on_device(fields, target, area_weights, hidden, w_in, w_out):
    anywhere = pl.BlockSpec(memory_space=pl.ANY)
    vmem = pl.BlockSpec(memory_space=pltpu.VMEM)
    dma = pltpu.SemaphoreType.DMA
    tile = (16, 128)
    loss, grad_hidden, grad_w1 = pl.pallas_call(
        forward_kernel,
        out_shape=(
            jax.ShapeDtypeStruct((1, 1), F32),
            pltpu.VMEM((LOCAL, HID), BF16),
            pltpu.VMEM((8, HID), F32),
        ),
        in_specs=[anywhere] * 6,
        out_specs=(pl.BlockSpec(memory_space=pltpu.SMEM), vmem, vmem),
        scratch_shapes=[
            pltpu.VMEM((HID, HID), BF16),
            pltpu.VMEM((CHANNELS, HID), BF16),
            pltpu.VMEM((LOCAL, HID), F32),
            pltpu.VMEM((LOCAL, HID), BF16),
            pltpu.VMEM((HID, HID), F32),
            pltpu.VMEM((2, MEMBERS, CHANNELS, SHARE), BF16),
            pltpu.VMEM((2, CHANNELS, SHARE), BF16),
            pltpu.VMEM((2, 1, SHARE), F32),
            pltpu.VMEM((2, MEMBERS, CHANNELS, SHARE), BF16),
            pltpu.VMEM((2, MEMBERS, CHANNELS, SHARE), BF16),
            pltpu.VMEM((BLOCKS, 2, 4, 4, 4) + tile, BF16),
            pltpu.VMEM((BLOCKS, 4, 4, 4) + tile, BF16),
            pltpu.VMEM((BLOCKS, 4, 4, 4) + tile, BF16),
            pltpu.VMEM((BLOCKS, 3, 4, 4) + tile, BF16),
            pltpu.VMEM((BLOCKS, 4, 4) + tile, BF16),
            pltpu.VMEM((BLOCKS, 3, 4) + tile, BF16),
            pltpu.VMEM((BLOCKS, 4) + tile, BF16),
            pltpu.VMEM((BLOCKS, 3) + tile, BF16),
            pltpu.VMEM((16, 128), F32),
            pltpu.VMEM((5, 8, 128), F32),
            pltpu.VMEM((10, 8, 128), F32),
            dma((2,)),
            dma((2, 3)),
            dma((LOCAL // CHUNK,)),
            dma((2, 2, MEMBERS - 1)),
            dma((2, 2, MEMBERS - 1)),
            dma((2, BLOCKS, 10)),
            dma((2, 10)),
        ],
        compiler_params=pltpu.CompilerParams(
            collective_id=0, has_side_effects=True, vmem_limit_bytes=52 * 2**20
        ),
        cost_estimate=pl.CostEstimate(
            flops=2 * LOCAL * HID * (3 * HID + CHANNELS),
            bytes_accessed=12 * 2**20,
            transcendentals=LOCAL * HID,
        ),
    )(fields, target, area_weights[None, :], hidden, w_in, w_out)
    return (loss[0, 0], grad_hidden[None], grad_w1)


def solution(mesh):
    return jax.shard_map(
        on_device,
        mesh=mesh,
        in_specs=(
            P("member", None, "space"),
            P(None, "space"),
            P("space"),
            P("member", "space", None),
            P(),
            P(),
        ),
        out_specs=(P(), P("member", "space", None), P(("member", "space"), None)),
        check_vma=False,
    )
```

```python
import functools
import math

import jax
import jax.numpy as jnp
from jax import lax
from jax.experimental import pallas as pl
from jax.experimental.pallas import tpu as pltpu
from jax.sharding import PartitionSpec as P

ALPHA_FAIR = 0.95
MEMBERS, SPACES = 8, 16
CHANNELS, LOCAL, HID = 100, 4096, 1024
ROOT = math.sqrt(2.0 / math.pi)
CUBIC = 0.044715
F32, BF16 = jnp.float32, jnp.bfloat16
MESH = pl.DeviceIdType.MESH

HALF = LOCAL // 2
SHARE = HALF // MEMBERS
CHUNK = 512

BLOCKS = 4
GROUPS = BLOCKS // 2
COLS = HID // BLOCKS


def gelu_slope(u):
    s = u * u
    t = jnp.tanh(u * (ROOT + (ROOT * CUBIC) * s))
    return 0.5 * (1.0 + t) + (1.0 - t * t) * (u * (0.5 * ROOT + (1.5 * ROOT * CUBIC) * s))


def sign(a, b):
    one, zero = jnp.ones((), a.dtype), jnp.zeros((), a.dtype)
    return jnp.where(a > b, one, jnp.where(a < b, -one, zero))


class Place:
    def __init__(self):
        self.member = lax.axis_index("member")
        self.space = lax.axis_index("space")
        x, z_hi = self.member // 2, self.member % 2
        y, z_lo = self.space // 4, (self.space // 2) % 2
        self.core = self.space % 2
        self.at = (x, y, z_hi * 2 + z_lo)

    def pick(self, place):
        axis = (2 * self.core + place) % 3
        return [(2 - axis) * (1 - axis) // 2, axis * (2 - axis), axis * (axis - 1) // 2]

    def slot(self, weights, d=0):
        return (sum(w * p for w, p in zip(weights, self.at)) + d) % 4

    def step(self, weights, d):
        at = [(p + w * d) % 4 for w, p in zip(weights, self.at)]
        return self.device(at, self.core)

    def in_plane(self, d, e):
        pairs = zip(self.at, self.pick(1), self.pick(2))
        return self.device([(p + v * d + w * e) % 4 for p, v, w in pairs], self.core)

    def device(self, at, core):
        x, y, z = at
        return {"member": x * 2 + z // 2, "space": (y * 2 + z % 2) * 2 + core}

    def along(self, axis, d):
        return self.step([int(axis == i) for i in range(3)], d)

    def other_core(self):
        return self.device(self.at, 1 - self.core)

    def other_member(self, d):
        return {"member": (self.member + d) % MEMBERS, "space": self.space}


def forward_kernel(
    fields, target, area, hidden, w_in, w_out,
    loss_out, held, grad_out,
    win, wout, slope, du, total,
    got, truth, weight, back, dx,
    sums, half0, sum1, part1, sum2, part2,
    lacc, lsum, lpart,
    local_sems, own_sems, hid_sems, field_sems, back_sems, rs_sems, plane_sems, loss_sems,
):
    here = Place()
    me = here.member
    count = MEMBERS
    fair = (1.0 - ALPHA_FAIR) / count
    coef = (1.0 - fair) / (count * (count - 1))

    def share(h, member):
        return pl.ds(pl.multiple_of(h * HALF + member * SHARE, SHARE), SHARE)

    def chunk(c):
        return pl.ds(pl.multiple_of(c * CHUNK, CHUNK), CHUNK)

    def load(c):
        rows = pl.ds(pl.multiple_of(c * CHUNK, CHUNK), CHUNK)
        return pltpu.make_async_copy(hidden.at[0, rows], held.at[rows], hid_sems.at[c])

    loads = [load(c) for c in range(LOCAL // CHUNK)]
    weights = [
        pltpu.make_async_copy(src, dst, local_sems.at[i])
        for i, (src, dst) in enumerate(((w_in, win), (w_out, wout)))
    ]
    def own_copies(h):
        return [
            pltpu.make_async_copy(src, dst, own_sems.at[h, i])
            for i, (src, dst) in enumerate((
                (fields.at[0, :, share(h, me)], got.at[h, me]),
                (target.at[:, share(h, me)], truth.at[h]),
                (area.at[:, share(h, me)], weight.at[h]),
            ))
        ]

    for copy in [weights[0], *loads[:2], *own_copies(0), *loads[2:], weights[1], *own_copies(1)]:
        copy.start()

    barrier = pltpu.get_barrier_semaphore()
    others = [here.other_member(d) for d in range(1, MEMBERS)]
    others += [here.other_core()]
    others += [here.along(1, d) for d in range(1, 4)]
    others += [here.along(2, d) for d in (1, 3)]
    others += [here.in_plane(d, e) for d in range(1, 4) for e in range(1, 4)]
    for device in others:
        pl.semaphore_signal(barrier, inc=1, device_id=device, device_id_type=MESH)

    def project(first, last):
        for c in range(first, last):
            loads[c].wait()

        def one_chunk(c, _):
            u = jnp.dot(held[chunk(c), :], win[...], preferred_element_type=F32)
            slope[chunk(c), :] = gelu_slope(u)
            return 0

        lax.fori_loop(first, last, one_chunk, 0)

    lacc[...] = jnp.zeros_like(lacc)
    pl.semaphore_wait(barrier, len(others))

    def exchange(h, sems, source, landed):
        return [
            pltpu.make_async_remote_copy(
                src_ref=source((me + d) % MEMBERS),
                dst_ref=landed.at[h, me],
                send_sem=sems.at[0, h, d - 1],
                recv_sem=sems.at[1, h, d - 1],
                device_id=here.other_member(d),
                device_id_type=MESH,
            )
            for d in range(1, MEMBERS)
        ]

    def arrive(h, sems, landed):
        for d in range(1, MEMBERS):
            slot = landed.at[h, (me + MEMBERS - d) % MEMBERS]
            pltpu.make_async_remote_copy(
                src_ref=slot, dst_ref=slot,
                send_sem=sems.at[0, h, d - 1], recv_sem=sems.at[1, h, d - 1],
                device_id=here.other_member(MEMBERS - d), device_id_type=MESH,
            ).wait_recv()

    def field_copies(h):
        return exchange(h, field_sems, lambda to: fields.at[0, :, share(h, to)], got)

    def back_copies(h):
        return exchange(h, back_sems, lambda to: back.at[h, to], dx)

    def own_back(h):
        return pltpu.make_async_copy(back.at[h, me], dx.at[h, me], own_sems.at[h, 0])

    def compare(h, start, rows):
        at = pl.ds(start, rows)
        for j in range(0, SHARE, 128):
            lanes = pl.ds(j, 128)
            x = [got[h, k, at, lanes] for k in range(MEMBERS)]
            y = truth[h, at, lanes]
            w = weight[h, :, lanes]
            pull = coef * w
            push = w / count
            signs = [None] * MEMBERS
            for a in range(MEMBERS):
                for b in range(a + 1, MEMBERS):
                    s = sign(x[a], x[b])
                    signs[a] = s if signs[a] is None else signs[a] + s
                    signs[b] = -s if signs[b] is None else signs[b] - s
            truth_ = y.astype(F32)
            spread, miss = 0.0, 0.0
            for k in range(MEMBERS):
                own_, tally = x[k].astype(F32), signs[k].astype(F32)
                spread = spread + own_ * tally
                miss = miss + jnp.abs(own_ - truth_)
                side = sign(own_, truth_)
                back[h, k, at, lanes] = (push * side - pull * tally).astype(BF16)
            lacc[pl.ds(0, rows), :] += w * (miss / count - coef * spread)

    def compare_half(h):
        for copy in own_copies(h):
            copy.wait()
        arrive(h, field_sems, got)

        def rows16(i, _):
            compare(h, pl.multiple_of(i * 16, 16), 16)
            return 0

        whole = CHANNELS // 16
        lax.fori_loop(0, whole, rows16, 0)
        compare(h, whole * 16, CHANNELS - whole * 16)
        for copy in (own_back(h), *back_copies(h)):
            copy.start()

    def upstream(h):
        own_back(h).wait()
        arrive(h, back_sems, dx)

        for k in range(MEMBERS):
            rows = pl.ds(h * HALF + k * SHARE, SHARE)
            dv = lax.dot_general(
                dx[h, k], wout[...], (((0,), (0,)), ((), ())), preferred_element_type=F32
            )
            du[rows, :] = (dv * slope[rows, :]).astype(BF16)

    def weight_grad(h, b):
        points, cols = pl.ds(h * HALF, HALF), pl.ds(b * COLS, COLS)
        return lax.dot_general(
            held[points, :], du[points, cols], (((0,), (0,)), ((), ())), preferred_element_type=F32
        )

    def pack(b, g):
        for r in range(HID // 8):
            core = r % 2
            at = (r // 32, (r // 4) % 4, ((r // 16) % 2) * 2 + (r // 2) % 2)
            i, j, k = (at[(2 * core + s) % 3] for s in range(3))
            rows = g[8 * r : 8 * r + 8]
            sums[b, core, i, j, k] = jnp.concatenate([rows[:, :128], rows[:, 128:]], 0).astype(BF16)

    def rs_copies(b, stage):
        if stage == 0:
            return [pltpu.make_async_remote_copy(
                src_ref=sums.at[b, 1 - here.core], dst_ref=half0.at[b],
                send_sem=rs_sems.at[0, b, 0], recv_sem=rs_sems.at[1, b, 0],
                device_id=here.other_core(), device_id_type=MESH,
            )]
        axis = here.pick(0)
        return [
            pltpu.make_async_remote_copy(
                src_ref=sum1.at[b, here.slot(axis, d)], dst_ref=part1.at[b, d - 1],
                send_sem=rs_sems.at[0, b, d], recv_sem=rs_sems.at[1, b, d],
                device_id=here.step(axis, d), device_id_type=MESH,
            )
            for d in (2, 1, 3)
        ]

    def rs_send(b, stage):
        for copy in rs_copies(b, stage):
            copy.start()

    def rs_sum(b, stage):
        for copy in rs_copies(b, stage):
            copy.wait_recv()
        if stage == 0:
            for p in range(4):
                sum1[b, p] = (
                    sums[b, here.core, p].astype(F32) + half0[b, p].astype(F32)
                ).astype(BF16)
            return
        value = sum1[b, here.slot(here.pick(0))].astype(F32)
        for d in range(3):
            value = value + part1[b, d].astype(F32)
        sum2[b // 2, :, :, b % 2] = value.astype(BF16)

    def plane_copies(g):
        v, w = here.pick(1), here.pick(2)
        return [
            pltpu.make_async_remote_copy(
                src_ref=sum2.at[g, here.slot(v, d), here.slot(w, e)],
                dst_ref=part2.at[g, d * 4 + e - 1],
                send_sem=plane_sems.at[0, g, d * 4 + e - 1],
                recv_sem=plane_sems.at[1, g, d * 4 + e - 1],
                device_id=here.in_plane(d, e),
                device_id_type=MESH,
            )
            for d in (2, 1, 3, 0)
            for e in (2, 1, 3, 0)
            if (d, e) != (0, 0)
        ]

    def plane_send(g):
        for copy in plane_copies(g):
            copy.start()

    def plane_sum(g):
        value = sum2[g, here.slot(here.pick(1)), here.slot(here.pick(2))].astype(F32)
        for copy in plane_copies(g):
            copy.wait_recv()
        for n in range(15):
            value = value + part2[g, n].astype(F32)
        value = value * (1.0 / math.sqrt(LOCAL * SPACES))
        for q in range(2):
            at = COLS * (2 * g + q)
            grad_out[:, pl.ds(at, 128)] = value[q, 0:8]
            grad_out[:, pl.ds(at + 128, 128)] = value[q, 8:16]

    def step(b, stage):
        rs_sum(b, stage)
        if stage == 0:
            rs_send(b, 1)

    def loss_copies(stage):
        copies = []
        for d in (1,) if stage == 0 else (1, 2, 3):
            k = d - 1 if stage == 0 else 1 + (stage - 1) * 3 + d - 1
            copies.append(pltpu.make_async_remote_copy(
                src_ref=lsum.at[stage],
                dst_ref=lpart.at[k],
                send_sem=loss_sems.at[0, k],
                recv_sem=loss_sems.at[1, k],
                device_id=here.other_core() if stage == 0 else here.along(stage - 1, d),
                device_id_type=MESH,
            ))
        return copies

    def loss_send(stage):
        for copy in loss_copies(stage):
            copy.start()

    def loss_step(stage):
        value = lsum[stage]
        first = 0 if stage == 0 else 1 + (stage - 1) * 3
        for d, copy in enumerate(loss_copies(stage)):
            copy.wait_recv()
            value = value + lpart[first + d]
        lsum[stage + 1] = value
        if stage < 3:
            loss_send(stage + 1)

    for copy in field_copies(0):
        copy.start()
    weights[0].wait()
    project(0, 3)
    for copy in field_copies(1):
        copy.start()
    project(3, 5)
    compare_half(0)
    project(5, 7)
    compare_half(1)
    project(7, 8)
    weights[1].wait()
    upstream(0)
    for b in range(BLOCKS):
        total[:, pl.ds(b * COLS, COLS)] = weight_grad(0, b)
    lsum[0] = lacc[0:8, :] + lacc[8:16, :]
    loss_send(0)
    upstream(1)
    for b in range(BLOCKS):
        pack(b, total[:, pl.ds(b * COLS, COLS)] + weight_grad(1, b))
        rs_send(b, 0)
        if b > 0:
            step(b - 1, 0)

    def first_plane():
        step(0, 1)
        step(1, 1)
        plane_send(0)

    def second_plane():
        step(2, 1)
        step(3, 1)
        plane_send(1)

    between = {
        0: lambda: (step(3, 0), loss_step(0)),
        2: lambda: (first_plane(), loss_step(1)),
        4: lambda: (second_plane(), loss_step(2)),
        7: lambda: plane_sum(0),
    }
    for c in range(LOCAL // CHUNK):
        held[chunk(c), :] = lax.dot_general(
            du[chunk(c), :], win[...], (((1,), (1,)), ((), ())), preferred_element_type=F32
        ).astype(BF16)
        if c in between:
            between[c]()
    loss_step(3)
    plane_sum(1)
    loss_out[0, 0] = jnp.sum(lsum[4]) / (CHANNELS * LOCAL * SPACES)

    for h in range(2):
        for copy in field_copies(h) + back_copies(h):
            copy.wait_send()
    for stage in range(4):
        for copy in loss_copies(stage):
            copy.wait_send()
    for b in range(BLOCKS):
        for copy in rs_copies(b, 0) + rs_copies(b, 1):
            copy.wait_send()
    for g in range(GROUPS):
        for copy in plane_copies(g):
            copy.wait_send()


def on_device(fields, target, area_weights, hidden, w_in, w_out):
    anywhere = pl.BlockSpec(memory_space=pl.ANY)
    vmem = pl.BlockSpec(memory_space=pltpu.VMEM)
    dma = pltpu.SemaphoreType.DMA
    tile = (16, 128)
    loss, grad_hidden, grad_w1 = pl.pallas_call(
        forward_kernel,
        out_shape=(
            jax.ShapeDtypeStruct((1, 1), F32),
            pltpu.VMEM((LOCAL, HID), BF16),
            pltpu.VMEM((8, HID), F32),
        ),
        in_specs=[anywhere] * 6,
        out_specs=(pl.BlockSpec(memory_space=pltpu.SMEM), vmem, vmem),
        scratch_shapes=[
            pltpu.VMEM((HID, HID), BF16),
            pltpu.VMEM((CHANNELS, HID), BF16),
            pltpu.VMEM((LOCAL, HID), F32),
            pltpu.VMEM((LOCAL, HID), BF16),
            pltpu.VMEM((HID, HID), F32),
            pltpu.VMEM((2, MEMBERS, CHANNELS, SHARE), BF16),
            pltpu.VMEM((2, CHANNELS, SHARE), BF16),
            pltpu.VMEM((2, 1, SHARE), F32),
            pltpu.VMEM((2, MEMBERS, CHANNELS, SHARE), BF16),
            pltpu.VMEM((2, MEMBERS, CHANNELS, SHARE), BF16),
            pltpu.VMEM((BLOCKS, 2, 4, 4, 4) + tile, BF16),
            pltpu.VMEM((BLOCKS, 4, 4, 4) + tile, BF16),
            pltpu.VMEM((BLOCKS, 4, 4, 4) + tile, BF16),
            pltpu.VMEM((BLOCKS, 3, 4, 4) + tile, BF16),
            pltpu.VMEM((GROUPS, 4, 4, 2) + tile, BF16),
            pltpu.VMEM((GROUPS, 15, 2) + tile, BF16),
            pltpu.VMEM((16, 128), F32),
            pltpu.VMEM((5, 8, 128), F32),
            pltpu.VMEM((10, 8, 128), F32),
            dma((2,)),
            dma((2, 3)),
            dma((LOCAL // CHUNK,)),
            dma((2, 2, MEMBERS - 1)),
            dma((2, 2, MEMBERS - 1)),
            dma((2, BLOCKS, 4)),
            dma((2, GROUPS, 15)),
            dma((2, 10)),
        ],
        compiler_params=pltpu.CompilerParams(
            collective_id=0, has_side_effects=True, vmem_limit_bytes=52 * 2**20
        ),
        cost_estimate=pl.CostEstimate(
            flops=2 * LOCAL * HID * (3 * HID + CHANNELS),
            bytes_accessed=12 * 2**20,
            transcendentals=LOCAL * HID,
        ),
    )(fields, target, area_weights[None, :], hidden, w_in, w_out)
    return (loss[0, 0], grad_hidden[None], grad_w1)


def solution(mesh):
    return jax.shard_map(
        on_device,
        mesh=mesh,
        in_specs=(
            P("member", None, "space"),
            P(None, "space"),
            P("space"),
            P("member", "space", None),
            P(),
            P(),
        ),
        out_specs=(P(), P("member", "space", None), P(("member", "space"), None)),
        check_vma=False,
    )
```

```python
import functools
import math

import jax
import jax.numpy as jnp
from jax import lax
from jax.experimental import pallas as pl
from jax.experimental.pallas import tpu as pltpu
from jax.sharding import PartitionSpec as P

ALPHA_FAIR = 0.95
MEMBERS, SPACES = 8, 16
CHANNELS, LOCAL, HID = 100, 4096, 1024
ROOT = math.sqrt(2.0 / math.pi)
CUBIC = 0.044715
F32, BF16 = jnp.float32, jnp.bfloat16
MESH = pl.DeviceIdType.MESH

HALF = LOCAL // 2
SHARE = HALF // MEMBERS
CHUNK = 512
STORES = 4

BLOCKS = 4
GROUPS = BLOCKS // 2
COLS = HID // BLOCKS


def gelu_slope(u):
    s = u * u
    t = jnp.tanh(u * (ROOT + (ROOT * CUBIC) * s))
    return 0.5 * (1.0 + t) + (1.0 - t * t) * (u * (0.5 * ROOT + (1.5 * ROOT * CUBIC) * s))


def sign(a, b):
    one, zero = jnp.ones((), a.dtype), jnp.zeros((), a.dtype)
    return jnp.where(a > b, one, jnp.where(a < b, -one, zero))


class Place:
    def __init__(self):
        self.member = lax.axis_index("member")
        self.space = lax.axis_index("space")
        x, z_hi = self.member // 2, self.member % 2
        y, z_lo = self.space // 4, (self.space // 2) % 2
        self.core = self.space % 2
        self.at = (x, y, z_hi * 2 + z_lo)

    def pick(self, place):
        axis = (2 * self.core + place) % 3
        return [(2 - axis) * (1 - axis) // 2, axis * (2 - axis), axis * (axis - 1) // 2]

    def slot(self, weights, d=0):
        return (sum(w * p for w, p in zip(weights, self.at)) + d) % 4

    def step(self, weights, d):
        at = [(p + w * d) % 4 for w, p in zip(weights, self.at)]
        return self.device(at, self.core)

    def in_plane(self, d, e):
        pairs = zip(self.at, self.pick(1), self.pick(2))
        return self.device([(p + v * d + w * e) % 4 for p, v, w in pairs], self.core)

    def device(self, at, core):
        x, y, z = at
        return {"member": x * 2 + z // 2, "space": (y * 2 + z % 2) * 2 + core}

    def along(self, axis, d):
        return self.step([int(axis == i) for i in range(3)], d)

    def other_core(self):
        return self.device(self.at, 1 - self.core)

    def other_member(self, d):
        return {"member": (self.member + d) % MEMBERS, "space": self.space}


def forward_kernel(
    fields, target, area, hidden, w_in, w_out,
    loss_out, held, grad_out,
    win, wout, slope, du, total,
    got, truth, weight, back, dx,
    sums, half0, sum1, part1, sum2, part2,
    lacc, lsum, lpart,
    local_sems, own_sems, hid_sems, field_sems, back_sems, rs_sems, plane_sems, loss_sems,
):
    here = Place()
    me = here.member
    count = MEMBERS
    fair = (1.0 - ALPHA_FAIR) / count
    coef = (1.0 - fair) / (count * (count - 1))

    def share(h, member):
        return pl.ds(pl.multiple_of(h * HALF + member * SHARE, SHARE), SHARE)

    def chunk(c):
        return pl.ds(pl.multiple_of(c * CHUNK, CHUNK), CHUNK)

    def load(c):
        rows = pl.ds(pl.multiple_of(c * CHUNK, CHUNK), CHUNK)
        return pltpu.make_async_copy(hidden.at[0, rows], held.at[rows], hid_sems.at[c])

    loads = [load(c) for c in range(LOCAL // CHUNK)]
    weights = [
        pltpu.make_async_copy(src, dst, local_sems.at[i])
        for i, (src, dst) in enumerate(((w_in, win), (w_out, wout)))
    ]
    def own_copies(h):
        return [
            pltpu.make_async_copy(src, dst, own_sems.at[h, i])
            for i, (src, dst) in enumerate((
                (fields.at[0, :, share(h, me)], got.at[h, me]),
                (target.at[:, share(h, me)], truth.at[h]),
                (area.at[:, share(h, me)], weight.at[h]),
            ))
        ]

    for copy in [weights[0], *loads[:2], *own_copies(0), *loads[2:], weights[1], *own_copies(1)]:
        copy.start()

    barrier = pltpu.get_barrier_semaphore()
    others = [here.other_member(d) for d in range(1, MEMBERS)]
    others += [here.other_core()]
    others += [here.along(1, d) for d in range(1, 4)]
    others += [here.along(2, d) for d in (1, 3)]
    others += [here.in_plane(d, e) for d in range(1, 4) for e in range(1, 4)]
    for device in others:
        pl.semaphore_signal(barrier, inc=1, device_id=device, device_id_type=MESH)

    def project(first, last):
        for c in range(first, last):
            loads[c].wait()

        rows = pl.ds(first * CHUNK, (last - first) * CHUNK)
        u = jnp.dot(held[rows, :], win[...], preferred_element_type=F32)
        slope[rows, :] = gelu_slope(u)

    lacc[...] = jnp.zeros_like(lacc)
    pl.semaphore_wait(barrier, len(others))

    def exchange(h, sems, source, landed):
        return [
            pltpu.make_async_remote_copy(
                src_ref=source((me + d) % MEMBERS),
                dst_ref=landed.at[h, me],
                send_sem=sems.at[0, h, d - 1],
                recv_sem=sems.at[1, h, d - 1],
                device_id=here.other_member(d),
                device_id_type=MESH,
            )
            for d in range(1, MEMBERS)
        ]

    def arrive(h, sems, landed):
        for d in range(1, MEMBERS):
            slot = landed.at[h, (me + MEMBERS - d) % MEMBERS]
            pltpu.make_async_remote_copy(
                src_ref=slot, dst_ref=slot,
                send_sem=sems.at[0, h, d - 1], recv_sem=sems.at[1, h, d - 1],
                device_id=here.other_member(MEMBERS - d), device_id_type=MESH,
            ).wait_recv()

    def field_copies(h):
        return exchange(h, field_sems, lambda to: fields.at[0, :, share(h, to)], got)

    def back_copies(h):
        return exchange(h, back_sems, lambda to: back.at[h, to], dx)

    def own_back(h):
        return pltpu.make_async_copy(back.at[h, me], dx.at[h, me], own_sems.at[h, 0])

    def compare(h, start, rows):
        at = pl.ds(start, rows)
        for j in range(0, SHARE, 128):
            lanes = pl.ds(j, 128)
            x = [got[h, k, at, lanes] for k in range(MEMBERS)]
            y = truth[h, at, lanes]
            w = weight[h, :, lanes]
            pull = coef * w
            push = w / count
            signs = [None] * MEMBERS
            for a in range(MEMBERS):
                for b in range(a + 1, MEMBERS):
                    s = sign(x[a], x[b])
                    signs[a] = s if signs[a] is None else signs[a] + s
                    signs[b] = -s if signs[b] is None else signs[b] - s
            truth_ = y.astype(F32)
            spread, miss = 0.0, 0.0
            for k in range(MEMBERS):
                own_, tally = x[k].astype(F32), signs[k].astype(F32)
                spread = spread + own_ * tally
                miss = miss + jnp.abs(own_ - truth_)
                side = sign(own_, truth_)
                back[h, k, at, lanes] = (push * side - pull * tally).astype(BF16)
            lacc[pl.ds(0, rows), :] += w * (miss / count - coef * spread)

    def compare_half(h):
        for copy in own_copies(h):
            copy.wait()
        arrive(h, field_sems, got)

        def rows16(i, _):
            compare(h, pl.multiple_of(i * 16, 16), 16)
            return 0

        whole = CHANNELS // 16
        lax.fori_loop(0, whole, rows16, 0)
        compare(h, whole * 16, CHANNELS - whole * 16)
        for copy in (own_back(h), *back_copies(h)):
            copy.start()

    def upstream(h):
        own_back(h).wait()
        arrive(h, back_sems, dx)

        for k in range(MEMBERS):
            rows = pl.ds(h * HALF + k * SHARE, SHARE)
            dv = lax.dot_general(
                dx[h, k], wout[...], (((0,), (0,)), ((), ())), preferred_element_type=F32
            )
            du[rows, :] = (dv * slope[rows, :]).astype(BF16)

    def weight_grad(h, b):
        points, cols = pl.ds(h * HALF, HALF), pl.ds(b * COLS, COLS)
        return lax.dot_general(
            held[points, :], du[points, cols], (((0,), (0,)), ((), ())), preferred_element_type=F32
        )

    def pack(b, g):
        for r in range(HID // 8):
            core = r % 2
            at = (r // 32, (r // 4) % 4, ((r // 16) % 2) * 2 + (r // 2) % 2)
            i, j, k = (at[(2 * core + s) % 3] for s in range(3))
            rows = g[8 * r : 8 * r + 8]
            sums[b, core, i, j, k] = jnp.concatenate([rows[:, :128], rows[:, 128:]], 0).astype(BF16)

    def rs_copies(b, stage):
        if stage == 0:
            return [pltpu.make_async_remote_copy(
                src_ref=sums.at[b, 1 - here.core], dst_ref=half0.at[b],
                send_sem=rs_sems.at[0, b, 0], recv_sem=rs_sems.at[1, b, 0],
                device_id=here.other_core(), device_id_type=MESH,
            )]
        axis = here.pick(0)
        return [
            pltpu.make_async_remote_copy(
                src_ref=sum1.at[b, here.slot(axis, d)], dst_ref=part1.at[b, d - 1],
                send_sem=rs_sems.at[0, b, d], recv_sem=rs_sems.at[1, b, d],
                device_id=here.step(axis, d), device_id_type=MESH,
            )
            for d in (2, 1, 3)
        ]

    def rs_send(b, stage):
        for copy in rs_copies(b, stage):
            copy.start()

    def rs_sum(b, stage):
        for copy in rs_copies(b, stage):
            copy.wait_recv()
        if stage == 0:
            for p in range(4):
                sum1[b, p] = (
                    sums[b, here.core, p].astype(F32) + half0[b, p].astype(F32)
                ).astype(BF16)
            return
        value = sum1[b, here.slot(here.pick(0))].astype(F32)
        for d in range(3):
            value = value + part1[b, d].astype(F32)
        sum2[b // 2, :, :, b % 2] = value.astype(BF16)

    def plane_copies(g):
        v, w = here.pick(1), here.pick(2)
        return [
            pltpu.make_async_remote_copy(
                src_ref=sum2.at[g, here.slot(v, d), here.slot(w, e)],
                dst_ref=part2.at[g, d * 4 + e - 1],
                send_sem=plane_sems.at[0, g, d * 4 + e - 1],
                recv_sem=plane_sems.at[1, g, d * 4 + e - 1],
                device_id=here.in_plane(d, e),
                device_id_type=MESH,
            )
            for d in (2, 1, 3, 0)
            for e in (2, 1, 3, 0)
            if (d, e) != (0, 0)
        ]

    def plane_send(g):
        for copy in plane_copies(g):
            copy.start()

    def plane_sum(g):
        value = sum2[g, here.slot(here.pick(1)), here.slot(here.pick(2))].astype(F32)
        for copy in plane_copies(g):
            copy.wait_recv()
        for n in range(15):
            value = value + part2[g, n].astype(F32)
        value = value * (1.0 / math.sqrt(LOCAL * SPACES))
        for q in range(2):
            at = COLS * (2 * g + q)
            grad_out[:, pl.ds(at, 128)] = value[q, 0:8]
            grad_out[:, pl.ds(at + 128, 128)] = value[q, 8:16]

    def step(b, stage):
        rs_sum(b, stage)
        if stage == 0:
            rs_send(b, 1)

    def loss_copies(stage):
        copies = []
        for d in (1,) if stage == 0 else (1, 2, 3):
            k = d - 1 if stage == 0 else 1 + (stage - 1) * 3 + d - 1
            copies.append(pltpu.make_async_remote_copy(
                src_ref=lsum.at[stage],
                dst_ref=lpart.at[k],
                send_sem=loss_sems.at[0, k],
                recv_sem=loss_sems.at[1, k],
                device_id=here.other_core() if stage == 0 else here.along(stage - 1, d),
                device_id_type=MESH,
            ))
        return copies

    def loss_send(stage):
        for copy in loss_copies(stage):
            copy.start()

    def loss_step(stage):
        value = lsum[stage]
        first = 0 if stage == 0 else 1 + (stage - 1) * 3
        for d, copy in enumerate(loss_copies(stage)):
            copy.wait_recv()
            value = value + lpart[first + d]
        lsum[stage + 1] = value
        if stage < 3:
            loss_send(stage + 1)

    for copy in field_copies(0):
        copy.start()
    weights[0].wait()
    project(0, 2)
    for copy in field_copies(1):
        copy.start()
    project(2, 4)
    project(4, 5)
    compare_half(0)
    project(5, 7)
    compare_half(1)
    project(7, 8)
    weights[1].wait()
    upstream(0)
    for b in range(BLOCKS):
        total[:, pl.ds(b * COLS, COLS)] = weight_grad(0, b)
    lsum[0] = lacc[0:8, :] + lacc[8:16, :]
    loss_send(0)
    upstream(1)
    for b in range(BLOCKS):
        pack(b, total[:, pl.ds(b * COLS, COLS)] + weight_grad(1, b))
        rs_send(b, 0)
        if b > 0:
            step(b - 1, 0)

    def first_plane():
        step(0, 1)
        step(1, 1)
        plane_send(0)

    def second_plane():
        step(2, 1)
        step(3, 1)
        plane_send(1)

    between = {
        0: lambda: (step(3, 0), loss_step(0)),
        2: lambda: (first_plane(), loss_step(1)),
        4: lambda: (second_plane(), loss_step(2)),
        7: lambda: plane_sum(0),
    }
    for c in range(LOCAL // CHUNK):
        held[chunk(c), :] = lax.dot_general(
            du[chunk(c), :], win[...], (((1,), (1,)), ((), ())), preferred_element_type=F32
        ).astype(BF16)
        if c in between:
            between[c]()
    loss_step(3)
    plane_sum(1)
    loss_out[0, 0] = jnp.sum(lsum[4]) / (CHANNELS * LOCAL * SPACES)

    for h in range(2):
        for copy in field_copies(h) + back_copies(h):
            copy.wait_send()
    for stage in range(4):
        for copy in loss_copies(stage):
            copy.wait_send()
    for b in range(BLOCKS):
        for copy in rs_copies(b, 0) + rs_copies(b, 1):
            copy.wait_send()
    for g in range(GROUPS):
        for copy in plane_copies(g):
            copy.wait_send()


def store_kernel(grad_hidden, grad_w1, hidden_out, w1_out, sems):
    copies = [pltpu.make_async_copy(grad_w1, w1_out, sems.at[STORES])]
    for i in range(STORES):
        rows = pl.ds(i * (LOCAL // STORES), LOCAL // STORES)
        copies.append(
            pltpu.make_async_copy(grad_hidden.at[rows], hidden_out.at[0, rows], sems.at[i])
        )
    for copy in copies:
        copy.start()
    for copy in copies:
        copy.wait()


def on_device(fields, target, area_weights, hidden, w_in, w_out):
    anywhere = pl.BlockSpec(memory_space=pl.ANY)
    vmem = pl.BlockSpec(memory_space=pltpu.VMEM)
    dma = pltpu.SemaphoreType.DMA
    tile = (16, 128)
    loss, grad_hidden, grad_w1 = pl.pallas_call(
        forward_kernel,
        out_shape=(
            jax.ShapeDtypeStruct((1, 1), F32),
            pltpu.VMEM((LOCAL, HID), BF16),
            pltpu.VMEM((8, HID), F32),
        ),
        in_specs=[anywhere] * 6,
        out_specs=(pl.BlockSpec(memory_space=pltpu.SMEM), vmem, vmem),
        scratch_shapes=[
            pltpu.VMEM((HID, HID), BF16),
            pltpu.VMEM((CHANNELS, HID), BF16),
            pltpu.VMEM((LOCAL, HID), F32),
            pltpu.VMEM((LOCAL, HID), BF16),
            pltpu.VMEM((HID, HID), F32),
            pltpu.VMEM((2, MEMBERS, CHANNELS, SHARE), BF16),
            pltpu.VMEM((2, CHANNELS, SHARE), BF16),
            pltpu.VMEM((2, 1, SHARE), F32),
            pltpu.VMEM((2, MEMBERS, CHANNELS, SHARE), BF16),
            pltpu.VMEM((2, MEMBERS, CHANNELS, SHARE), BF16),
            pltpu.VMEM((BLOCKS, 2, 4, 4, 4) + tile, BF16),
            pltpu.VMEM((BLOCKS, 4, 4, 4) + tile, BF16),
            pltpu.VMEM((BLOCKS, 4, 4, 4) + tile, BF16),
            pltpu.VMEM((BLOCKS, 3, 4, 4) + tile, BF16),
            pltpu.VMEM((GROUPS, 4, 4, 2) + tile, BF16),
            pltpu.VMEM((GROUPS, 15, 2) + tile, BF16),
            pltpu.VMEM((16, 128), F32),
            pltpu.VMEM((5, 8, 128), F32),
            pltpu.VMEM((10, 8, 128), F32),
            dma((2,)),
            dma((2, 3)),
            dma((LOCAL // CHUNK,)),
            dma((2, 2, MEMBERS - 1)),
            dma((2, 2, MEMBERS - 1)),
            dma((2, BLOCKS, 4)),
            dma((2, GROUPS, 15)),
            dma((2, 10)),
        ],
        compiler_params=pltpu.CompilerParams(
            collective_id=0, has_side_effects=True, vmem_limit_bytes=52 * 2**20
        ),
        cost_estimate=pl.CostEstimate(
            flops=2 * LOCAL * HID * (3 * HID + CHANNELS),
            bytes_accessed=12 * 2**20,
            transcendentals=LOCAL * HID,
        ),
    )(fields, target, area_weights[None, :], hidden, w_in, w_out)
    vmem_in = [pltpu.with_memory_space_constraint(a, pltpu.VMEM) for a in (grad_hidden, grad_w1)]
    grad_hidden, grad_w1 = pl.pallas_call(
        store_kernel,
        out_shape=(
            jax.ShapeDtypeStruct((1, LOCAL, HID), BF16),
            jax.ShapeDtypeStruct((8, HID), F32),
        ),
        in_specs=[vmem, vmem],
        out_specs=(anywhere, anywhere),
        scratch_shapes=[dma((STORES + 1,))],
        compiler_params=pltpu.CompilerParams(vmem_limit_bytes=2**20),
    )(*vmem_in)
    return (loss[0, 0], grad_hidden, grad_w1)


def solution(mesh):
    return jax.shard_map(
        on_device,
        mesh=mesh,
        in_specs=(
            P("member", None, "space"),
            P(None, "space"),
            P("space"),
            P("member", "space", None),
            P(),
            P(),
        ),
        out_specs=(P(), P("member", "space", None), P(("member", "space"), None)),
        check_vma=False,
    )
```
